32 devices in a mesh: inner: 8 (over y, x, core), outer: 4 (over z).
Axes of the slice: x: 2, y: 2, z: 4, core: 2. Of those that a mesh axis runs over, the one named last changes fastest.
Arguments:
- grad_first: bfloat16 [4, 8, 8, 4, 6, 128], P('outer', 'inner'), may hold values from -1 to 1
- grad_second: bfloat16 [4, 8, 8, 4, 6, 128], P('outer', 'inner'), may hold values from -1 to 1
- master: float32 [2, 8, 4, 6, 128], P(None, 'inner', 'outer'), may hold values from -0.12 to 0.12
- first_moment: float32 [2, 8, 4, 6, 128], P(None, 'inner', 'outer'), may hold values from -1.2 to 1.2
- second_moment: float32 [2, 8, 4, 6, 128], P(None, 'inner', 'outer'), may hold values from 0.01 to 1
Outputs:
- new_master: float32 [2, 8, 4, 6, 128], P(None, 'inner', 'outer')
- new_first: float32 [2, 8, 4, 6, 128], P(None, 'inner', 'outer')
- new_second: float32 [2, 8, 4, 6, 128], P(None, 'inner', 'outer')
- weight_codes: bfloat16 [2, 8, 4, 6, 128], P(None, None, 'outer')
- weight_scales: bfloat16 [2, 8, 4, 6], P(None, None, 'outer')
The draws below stay inside these ranges and needn't reach their ends.
All inputs are finite; a program needn't handle non-finite values.
Results may differ from the reference program's by a relative error of at most 0.012.
Values may be sent and summed in bfloat16 or wider, within the bound.
A program may use at most 64 MiB of HBM per device.

```python
import math
import jax
import jax.numpy as jnp
from jax import lax

QB = 128
ROWS_DEV = 6
N_INNER = 8
N_OUTER = 4


def spread_blocks(key, spike):
    shape = (N_OUTER, N_INNER, N_INNER, N_OUTER, ROWS_DEV, QB)
    base = jax.random.normal(jax.random.fold_in(key, 11), shape, jnp.float32)
    order = jax.random.permutation(jax.random.fold_in(key, 12), N_INNER)
    paired = (order[:, None] == jnp.arange(N_INNER)[None, :]).astype(jnp.float32)
    factor = 1.0 + (spike - 1.0) * paired
    values = base * factor[None, :, :, None, None, None] * (N_INNER * N_OUTER) ** (-0.5)
    return jnp.clip(values, -1.0, 1.0)


def draw_grad_first(key, part):
    key = jax.random.fold_in(key, 1)
    return spread_blocks(key, 4.0).astype(jnp.bfloat16)


def draw_grad_second(key, part):
    key = jax.random.fold_in(key, 2)
    return spread_blocks(key, 4.0).astype(jnp.bfloat16)


def level_of(key, extent, split, least, high):
    level = 1.0
    for position, blocks in split:
        draws = jax.random.uniform(jax.random.fold_in(jax.random.fold_in(key, 6), position), (blocks,), jnp.float32, least / len(split), high / len(split))
        level = level * jnp.repeat(jnp.exp(draws), extent[position] // blocks).reshape((-1,) + (1,) * (len(extent) - 1 - position))
    return level


def normal_values(rng, dims, deviation, most, split=(), kind=jnp.bfloat16):
    entries = jax.random.normal(rng, dims, jnp.float32) * deviation
    if len(split) > 0:
        entries = level_of(rng, dims, split, -0.22, 0.18) * entries
    return jnp.clip(entries, min=-most, max=most).astype(kind)


def setup_inputs(seed: int = 0) -> dict:
    keys = jax.random.split(jax.random.key(seed), 6)
    return {
        "grad_first": draw_grad_first(jax.random.fold_in(keys[5], 71), 0),
        "grad_second": draw_grad_second(jax.random.fold_in(keys[5], 71), 0),
        "master": normal_values(keys[2], (2, N_INNER, N_OUTER, ROWS_DEV, QB), 0.02, 0.12, ((1, 8), (2, 4)), jnp.float32),
        "first_moment": normal_values(keys[3], (2, N_INNER, N_OUTER, ROWS_DEV, QB), 0.2, 1.2, ((1, 8), (2, 4)), jnp.float32),
        "second_moment": jnp.clip(jnp.exp(math.log(1.0) - 4.6051702 * jax.random.uniform(keys[4], (2, N_INNER, N_OUTER, ROWS_DEV, QB), jnp.float32) ** level_of(keys[4], (2, N_INNER, N_OUTER, ROWS_DEV, QB), ((1, 8), (2, 4)), -0.2, 0.2)), 0.01, 1.0),
    }


EPSILON = 1e-06
CODE_RANGE = 448.0
BETA_ONE = 0.9
BETA_TWO = 0.95
LEARN_RATE = 0.01
WEIGHT_DECAY = 0.1
ADAM_EPSILON = 1e-08
steps_done = 10.0

def quantize(values):
    widened = values.astype(jnp.float32)
    block_scale = ((lax.optimization_barrier(jnp.max(jnp.abs(widened), axis=-1)) + EPSILON) / CODE_RANGE).astype(jnp.bfloat16)
    quant_codes = (widened / block_scale.astype(jnp.float32)[..., None]).astype(jnp.bfloat16)
    return (quant_codes, block_scale)

def restore(quant_codes, block_scale):
    return quant_codes.astype(jnp.float32) * block_scale.astype(jnp.float32)[..., None]

def adamw(reduced, params, first, second):
    first_next = BETA_ONE * first + (1.0 - BETA_ONE) * reduced
    second_next = BETA_TWO * second + (1.0 - BETA_TWO) * reduced * reduced
    first_hat = first_next / (1.0 - BETA_ONE ** steps_done)
    second_hat = second_next / (1.0 - BETA_TWO ** steps_done)
    params_next = params - LEARN_RATE * (first_hat / (jnp.sqrt(second_hat) + ADAM_EPSILON) + WEIGHT_DECAY * params)
    return (params_next, first_next, second_next)

def group_partial(group_grads):
    quant_codes, block_scale = quantize(group_grads)
    return lax.optimization_barrier(jnp.sum(restore(quant_codes, block_scale), axis=0))

def reference(grad_first, grad_second, master, first_moment, second_moment):
    masters, firsts, seconds, all_codes, all_scales = ([], [], [], [], [])
    for bucket, gradient in enumerate((grad_first, grad_second)):
        partials = lax.map(group_partial, gradient)
        codes_two, scale_two = quantize(partials)
        reduced = lax.optimization_barrier(jnp.sum(restore(codes_two, scale_two), axis=0))
        params_next, first_next, second_next = adamw(reduced, master[bucket], first_moment[bucket], second_moment[bucket])
        weight_code, weight_scale = quantize(params_next)
        masters.append(params_next)
        firsts.append(first_next)
        seconds.append(second_next)
        all_codes.append(weight_code)
        all_scales.append(weight_scale)
    return (jnp.stack(masters), jnp.stack(firsts), jnp.stack(seconds), jnp.stack(all_codes), jnp.stack(all_scales))
```

```python
import functools

import jax
import jax.numpy as jnp
from jax import lax
from jax.experimental import pallas as pl
from jax.experimental.pallas import tpu as pltpu
from jax.sharding import PartitionSpec as P

EPSILON = 1e-06
CODE_RANGE = 448.0
BETA_ONE = 0.9
BETA_TWO = 0.95
LEARN_RATE = 0.01
WEIGHT_DECAY = 0.1
ADAM_EPSILON = 1e-08
steps_done = 10.0
MESH = pl.DeviceIdType.MESH


def quantize(widened):
    most = jnp.max(jnp.abs(widened), axis=-1, keepdims=True)
    scale = ((most + EPSILON) / CODE_RANGE).astype(jnp.bfloat16).astype(jnp.float32)
    codes = (widened / scale).astype(jnp.bfloat16).astype(jnp.float32)
    return codes, scale


def requantized(widened):
    codes, scale = quantize(widened)
    return codes * scale


def adamw(reduced, params, first, second):
    first_next = BETA_ONE * first + (1.0 - BETA_ONE) * reduced
    second_next = BETA_TWO * second + (1.0 - BETA_TWO) * reduced * reduced
    first_hat = first_next / (1.0 - BETA_ONE**steps_done)
    second_hat = second_next / (1.0 - BETA_TWO**steps_done)
    params_next = params - LEARN_RATE * (
        first_hat / (jnp.sqrt(second_hat) + ADAM_EPSILON) + WEIGHT_DECAY * params
    )
    return (params_next, first_next, second_next)


def loop(count, body, carry):
    if count <= 8:
        for step in range(1, count):
            carry = body(step, carry)
        return carry
    return lax.fori_loop(1, count, body, carry)


def kernel(
    n_inner, n_outer, rows, padded,
    grad_first, grad_second, master, first_moment, second_moment,
    new_master, new_first, new_second, weight_codes, weight_scales,
    stage, terms, partial, sums, packed, state,
    load_sem, send_one, recv_one, send_two, recv_two, send_three, recv_three,
):
    inner = lax.axis_index("inner")
    outer = lax.axis_index("outer")
    both = 2 * rows
    width = stage.shape[-1]

    def inner_peer(step):
        return lax.rem(inner + step, n_inner)

    def outer_peer(step):
        return lax.rem(outer + step, n_outer)

    barrier = pltpu.get_barrier_semaphore()

    def greet_inner(step, carry):
        pl.semaphore_signal(barrier, inc=1, device_id={"inner": inner_peer(step)}, device_id_type=MESH)
        return carry

    def greet_outer(step, carry):
        pl.semaphore_signal(barrier, inc=1, device_id={"outer": outer_peer(step)}, device_id_type=MESH)
        return carry

    loop(n_inner, greet_inner, 0)
    loop(n_outer, greet_outer, 0)
    grads = [
        pltpu.make_async_copy(ref, stage.at[:, bucket], load_sem.at[bucket])
        for bucket, ref in enumerate((grad_first, grad_second))
    ]
    states = [
        pltpu.make_async_copy(ref, state.at[place], load_sem.at[2 + place])
        for place, ref in enumerate((master, first_moment, second_moment))
    ]
    for copy in grads + states:
        copy.start()
    for copy in grads:
        copy.wait()
    pl.semaphore_wait(barrier, n_inner - 1 + n_outer - 1)

    def term_copy(step):
        return pltpu.make_async_remote_copy(
            src_ref=stage.at[inner_peer(step)],
            dst_ref=terms.at[step],
            send_sem=send_one.at[step],
            recv_sem=recv_one.at[step],
            device_id={"inner": inner_peer(step)},
            device_id_type=MESH,
        )

    def send_term(step, carry):
        term_copy(step).start()
        return carry

    loop(n_inner, send_term, 0)
    total = requantized(stage[inner].astype(jnp.float32))

    def add_term(step, total):
        term_copy(step).wait_recv()
        return total + requantized(terms[step].astype(jnp.float32))

    total = loop(n_inner, add_term, total).reshape(both, n_outer, width)
    for group in range(n_outer):
        partial[group] = total[:, group]

    def sum_copy(step):
        return pltpu.make_async_remote_copy(
            src_ref=partial.at[outer_peer(step)],
            dst_ref=sums.at[step],
            send_sem=send_two.at[step],
            recv_sem=recv_two.at[step],
            device_id={"outer": outer_peer(step)},
            device_id_type=MESH,
        )

    def send_sum(step, carry):
        sum_copy(step).start()
        return carry

    loop(n_outer, send_sum, 0)
    reduced = requantized(partial[outer])
    for copy in states:
        copy.wait()
    params, first, second = (state[place, :, 0] for place in range(3))

    def add_sum(step, reduced):
        sum_copy(step).wait_recv()
        return reduced + requantized(sums[step])

    reduced = loop(n_outer, add_sum, reduced)

    params_next, first_next, second_next = adamw(reduced, params, first, second)
    codes, scale = quantize(params_next)
    lane = lax.broadcasted_iota(jnp.int32, (both, width), 1)
    row = lax.broadcasted_iota(jnp.int32, (both, width), 0)
    across = [
        jnp.sum(jnp.where(lane + bucket * rows == row, jnp.where(lane < rows, scale, 0.0), 0.0), axis=0, keepdims=True)
        for bucket in range(2)
    ]
    fill = jnp.zeros((padded - both - 2, width), jnp.float32)
    packed[inner] = jnp.concatenate([codes] + across + [fill], axis=0).astype(jnp.bfloat16)

    def weight_copy(step):
        return pltpu.make_async_remote_copy(
            src_ref=packed.at[inner],
            dst_ref=packed.at[inner],
            send_sem=send_three.at[step],
            recv_sem=recv_three.at[step],
            device_id={"inner": inner_peer(step)},
            device_id_type=MESH,
        )

    def send_weight(step, carry):
        weight_copy(step).start()
        return carry

    loop(n_inner, send_weight, 0)
    new_master[:, 0] = params_next
    new_first[:, 0] = first_next
    new_second[:, 0] = second_next

    def finish_terms(step, carry):
        term_copy(step).wait_send()
        return carry

    def finish_sums(step, carry):
        sum_copy(step).wait_send()
        return carry

    def finish_weights(step, carry):
        weight_copy(step).wait()
        return carry

    loop(n_inner, finish_terms, 0)
    loop(n_outer, finish_sums, 0)
    loop(n_inner, finish_weights, 0)
    gathered = packed[...].astype(jnp.float32)
    for place in range(both):
        weight_codes[place] = gathered[:, place].astype(jnp.bfloat16)
    for bucket in range(2):
        turned = jnp.transpose(gathered[:, both + bucket])
        weight_scales[:, bucket] = turned[:rows].astype(jnp.bfloat16)


def place_kernel(*refs):
    sources, results, sem = refs[:5], refs[5:10], refs[10]
    copies = [
        pltpu.make_async_copy(source, result, sem.at[place])
        for place, (source, result) in enumerate(zip(sources, results))
    ]
    for copy in copies:
        copy.start()
    for copy in copies:
        copy.wait()


def local(n_inner, n_outer, grad_first, grad_second, master, first_moment, second_moment):
    rows, width = grad_first.shape[-2:]
    both = 2 * rows
    padded = 16 * ((both + 2 + 15) // 16)
    owned = jax.ShapeDtypeStruct((both, 1, width), jnp.float32)
    shapes = (
        owned,
        owned,
        owned,
        jax.ShapeDtypeStruct((both, n_inner, width), jnp.bfloat16),
        jax.ShapeDtypeStruct((rows, 2, n_inner), jnp.bfloat16),
    )
    hbm = pl.BlockSpec(memory_space=pl.ANY)
    vmem = pl.BlockSpec(memory_space=pltpu.VMEM)
    dma = pltpu.SemaphoreType.DMA
    results = pl.pallas_call(
        functools.partial(kernel, n_inner, n_outer, rows, padded),
        out_shape=shapes,
        in_specs=[pl.BlockSpec(memory_space=pltpu.HBM)] * 5,
        out_specs=(vmem,) * 5,
        scratch_shapes=[
            pltpu.VMEM((n_inner, 2, rows, n_outer, width), jnp.bfloat16),
            pltpu.VMEM((n_inner, 2, rows, n_outer, width), jnp.bfloat16),
            pltpu.VMEM((n_outer, both, width), jnp.float32),
            pltpu.VMEM((n_outer, both, width), jnp.float32),
            pltpu.VMEM((n_inner, padded, width), jnp.bfloat16),
            pltpu.VMEM((3, both, 1, width), jnp.float32),
            dma((5,)),
            dma((n_inner,)),
            dma((n_inner,)),
            dma((n_outer,)),
            dma((n_outer,)),
            dma((n_inner,)),
            dma((n_inner,)),
        ],
        compiler_params=pltpu.CompilerParams(
            collective_id=0, has_side_effects=True
        ),
        name="reduce_update_gather",
    )(
        jnp.swapaxes(grad_first[0, 0], 1, 2),
        jnp.swapaxes(grad_second[0, 0], 1, 2),
        master.reshape(both, 1, width),
        first_moment.reshape(both, 1, width),
        second_moment.reshape(both, 1, width),
    )
    results = pl.pallas_call(
        place_kernel,
        out_shape=shapes,
        in_specs=[vmem] * 5,
        out_specs=(hbm,) * 5,
        scratch_shapes=[dma((5,))],
        name="place_results",
    )(*results)
    new_master, new_first, new_second, weight_codes, weight_scales = results
    state_shape = (2, 1, 1, rows, width)
    return (
        new_master.reshape(state_shape),
        new_first.reshape(state_shape),
        new_second.reshape(state_shape),
        jnp.swapaxes(weight_codes.reshape(2, rows, n_inner, width), 1, 2)[:, :, None],
        jnp.transpose(weight_scales, (1, 2, 0))[:, :, None],
    )


def solution(mesh):
    return jax.shard_map(
        functools.partial(local, mesh.shape["inner"], mesh.shape["outer"]),
        mesh=mesh,
        in_specs=(
            P("outer", "inner", None, None, None, None),
            P("outer", "inner", None, None, None, None),
            P(None, "inner", "outer", None, None),
            P(None, "inner", "outer", None, None),
            P(None, "inner", "outer", None, None),
        ),
        out_specs=(
            P(None, "inner", "outer", None, None),
            P(None, "inner", "outer", None, None),
            P(None, "inner", "outer", None, None),
            P(None, None, "outer", None, None),
            P(None, None, "outer", None),
        ),
        check_vma=False,
    )
```

```python
import functools

import jax
import jax.numpy as jnp
from jax import lax
from jax.experimental import pallas as pl
from jax.experimental.pallas import tpu as pltpu
from jax.sharding import PartitionSpec as P

EPSILON = 1e-06
CODE_RANGE = 448.0
BETA_ONE = 0.9
BETA_TWO = 0.95
LEARN_RATE = 0.01
WEIGHT_DECAY = 0.1
ADAM_EPSILON = 1e-08
steps_done = 10.0
MESH = pl.DeviceIdType.MESH


def quantize(widened):
    most = jnp.max(jnp.abs(widened), axis=-1, keepdims=True)
    scale = ((most + EPSILON) / CODE_RANGE).astype(jnp.bfloat16).astype(jnp.float32)
    codes = (widened / scale).astype(jnp.bfloat16).astype(jnp.float32)
    return codes, scale


def requantized(widened):
    codes, scale = quantize(widened)
    return codes * scale


def adamw(reduced, params, first, second):
    first_next = BETA_ONE * first + (1.0 - BETA_ONE) * reduced
    second_next = BETA_TWO * second + (1.0 - BETA_TWO) * reduced * reduced
    first_hat = first_next / (1.0 - BETA_ONE**steps_done)
    second_hat = second_next / (1.0 - BETA_TWO**steps_done)
    params_next = params - LEARN_RATE * (
        first_hat / (jnp.sqrt(second_hat) + ADAM_EPSILON) + WEIGHT_DECAY * params
    )
    return (params_next, first_next, second_next)


def loop(count, body, carry):
    if count <= 8:
        for step in range(1, count):
            carry = body(step, carry)
        return carry
    return lax.fori_loop(1, count, body, carry)


def arrived(slots, count, sem):
    others = slots.at[pl.ds(1, count - 1)]
    pltpu.make_async_copy(others, others, sem).wait()


def kernel(
    n_inner, n_outer, rows, padded,
    grad_first, grad_second, master, first_moment, second_moment,
    new_master, new_first, new_second, weight_codes, weight_scales,
    stage, terms, spread, partial, sums, packed, lined, state,
    load_sem, send_one, recv_one, send_two, recv_two, send_three, recv_three,
):
    inner = lax.axis_index("inner")
    outer = lax.axis_index("outer")
    both = 2 * rows
    width = stage.shape[-1]

    def inner_peer(step):
        return lax.rem(inner + step, n_inner)

    def outer_peer(step):
        return lax.rem(outer + step, n_outer)

    grads = [
        pltpu.make_async_copy(ref, stage.at[:, bucket], load_sem.at[bucket])
        for bucket, ref in enumerate((grad_first, grad_second))
    ]
    states = [
        pltpu.make_async_copy(ref, state.at[place], load_sem.at[2 + place])
        for place, ref in enumerate((master, first_moment, second_moment))
    ]
    for copy in grads:
        copy.start()

    barrier = pltpu.get_barrier_semaphore()

    def greet_inner(step, carry):
        pl.semaphore_signal(barrier, inc=1, device_id={"inner": inner_peer(step)}, device_id_type=MESH)
        return carry

    def greet_outer(step, carry):
        pl.semaphore_signal(barrier, inc=1, device_id={"outer": outer_peer(step)}, device_id_type=MESH)
        return carry

    loop(n_inner, greet_inner, 0)
    loop(n_outer, greet_outer, 0)
    for copy in states:
        copy.start()
    for copy in grads:
        copy.wait()
    pl.semaphore_wait(barrier, n_inner - 1 + n_outer - 1)

    def send_term(step, carry):
        pltpu.make_async_remote_copy(
            src_ref=stage.at[inner_peer(step)],
            dst_ref=terms.at[step],
            send_sem=send_one,
            recv_sem=recv_one,
            device_id={"inner": inner_peer(step)},
            device_id_type=MESH,
        ).start()
        return carry

    loop(n_inner, send_term, 0)
    total = requantized(stage[inner].astype(jnp.float32))
    arrived(terms, n_inner, recv_one)
    if n_inner <= 8:
        total = total + jnp.sum(requantized(terms[1:].astype(jnp.float32)), axis=0)
    else:
        total = lax.fori_loop(
            1, n_inner, lambda step, total: total + requantized(terms[step].astype(jnp.float32)), total
        )
    spread[...] = total.reshape(both * n_outer, width)
    for group in range(n_outer):
        partial[group] = spread[pl.ds(group, both, stride=n_outer), :]

    def send_sum(step, carry):
        pltpu.make_async_remote_copy(
            src_ref=partial.at[outer_peer(step)],
            dst_ref=sums.at[step],
            send_sem=send_two,
            recv_sem=recv_two,
            device_id={"outer": outer_peer(step)},
            device_id_type=MESH,
        ).start()
        return carry

    loop(n_outer, send_sum, 0)
    own = requantized(partial[outer])
    for copy in states:
        copy.wait()
    params, first, second = (state[place, :, 0] for place in range(3))
    arrived(sums, n_outer, recv_two)
    reduced = own + jnp.sum(requantized(sums[1:]), axis=0)

    params_next, first_next, second_next = adamw(reduced, params, first, second)
    codes, scale = quantize(params_next)
    lane = lax.broadcasted_iota(jnp.int32, (both, width), 1)
    across = jnp.where(lane == inner, scale, 0.0)
    fill = jnp.zeros((padded - 2 * both, width), jnp.float32)
    packed[inner] = jnp.concatenate([codes, across, fill], axis=0).astype(jnp.bfloat16)

    def send_weight(step, carry):
        pltpu.make_async_remote_copy(
            src_ref=packed.at[inner],
            dst_ref=packed.at[inner],
            send_sem=send_three,
            recv_sem=recv_three,
            device_id={"inner": inner_peer(step)},
            device_id_type=MESH,
        ).start()
        return carry

    loop(n_inner, send_weight, 0)
    new_master[:, 0] = params_next
    new_first[:, 0] = first_next
    new_second[:, 0] = second_next
    arrived(terms, n_inner, send_one)
    arrived(sums, n_outer, send_two)
    arrived(packed, n_inner, send_three)
    arrived(packed, n_inner, recv_three)
    gathered = packed[...].astype(jnp.float32)
    lined[...] = gathered.reshape(n_inner * padded, width)
    for place in range(both):
        weight_codes[place] = lined[pl.ds(place, n_inner, stride=padded), :].astype(jnp.bfloat16)
    scales = jnp.sum(gathered[:, both : 2 * both], axis=0)
    for bucket in range(2):
        weight_scales[:, bucket] = scales[bucket * rows : (bucket + 1) * rows, :n_inner].astype(jnp.bfloat16)


def place_kernel(*refs):
    sources, results, sem = refs[:5], refs[5:10], refs[10]
    copies = [
        pltpu.make_async_copy(source, result, sem.at[place])
        for place, (source, result) in enumerate(zip(sources, results))
    ]
    for copy in copies:
        copy.start()
    for copy in copies:
        copy.wait()


def local(n_inner, n_outer, grad_first, grad_second, master, first_moment, second_moment):
    rows, width = grad_first.shape[-2:]
    both = 2 * rows
    padded = 16 * ((2 * both + 15) // 16)
    owned = jax.ShapeDtypeStruct((both, 1, width), jnp.float32)
    shapes = (
        owned,
        owned,
        owned,
        jax.ShapeDtypeStruct((both, n_inner, width), jnp.bfloat16),
        jax.ShapeDtypeStruct((rows, 2, n_inner), jnp.bfloat16),
    )
    hbm = pl.BlockSpec(memory_space=pl.ANY)
    vmem = pl.BlockSpec(memory_space=pltpu.VMEM)
    dma = pltpu.SemaphoreType.DMA
    results = pl.pallas_call(
        functools.partial(kernel, n_inner, n_outer, rows, padded),
        out_shape=shapes,
        in_specs=[pl.BlockSpec(memory_space=pltpu.HBM)] * 5,
        out_specs=(vmem,) * 5,
        scratch_shapes=[
            pltpu.VMEM((n_inner, 2, rows * n_outer, width), jnp.bfloat16),
            pltpu.VMEM((n_inner, 2, rows * n_outer, width), jnp.bfloat16),
            pltpu.VMEM((both * n_outer, width), jnp.float32),
            pltpu.VMEM((n_outer, both, width), jnp.float32),
            pltpu.VMEM((n_outer, both, width), jnp.float32),
            pltpu.VMEM((n_inner, padded, width), jnp.bfloat16),
            pltpu.VMEM((n_inner * padded, width), jnp.float32),
            pltpu.VMEM((3, both, 1, width), jnp.float32),
            dma((5,)),
            dma, dma, dma, dma, dma, dma,
        ],
        compiler_params=pltpu.CompilerParams(
            collective_id=0, has_side_effects=True
        ),
        name="reduce_update_gather",
    )(
        jnp.swapaxes(grad_first[0, 0], 1, 2).reshape(n_inner, rows * n_outer, width),
        jnp.swapaxes(grad_second[0, 0], 1, 2).reshape(n_inner, rows * n_outer, width),
        master.reshape(both, 1, width),
        first_moment.reshape(both, 1, width),
        second_moment.reshape(both, 1, width),
    )
    results = pl.pallas_call(
        place_kernel,
        out_shape=shapes,
        in_specs=[vmem] * 5,
        out_specs=(hbm,) * 5,
        scratch_shapes=[dma((5,))],
        name="place_results",
    )(*results)
    new_master, new_first, new_second, weight_codes, weight_scales = results
    state_shape = (2, 1, 1, rows, width)
    return (
        new_master.reshape(state_shape),
        new_first.reshape(state_shape),
        new_second.reshape(state_shape),
        jnp.swapaxes(weight_codes.reshape(2, rows, n_inner, width), 1, 2)[:, :, None],
        jnp.transpose(weight_scales, (1, 2, 0))[:, :, None],
    )


def solution(mesh):
    return jax.shard_map(
        functools.partial(local, mesh.shape["inner"], mesh.shape["outer"]),
        mesh=mesh,
        in_specs=(
            P("outer", "inner", None, None, None, None),
            P("outer", "inner", None, None, None, None),
            P(None, "inner", "outer", None, None),
            P(None, "inner", "outer", None, None),
            P(None, "inner", "outer", None, None),
        ),
        out_specs=(
            P(None, "inner", "outer", None, None),
            P(None, "inner", "outer", None, None),
            P(None, "inner", "outer", None, None),
            P(None, None, "outer", None, None),
            P(None, None, "outer", None),
        ),
        check_vma=False,
    )
```

```python
import functools

import jax
import jax.numpy as jnp
from jax import lax
from jax.experimental import pallas as pl
from jax.experimental.pallas import tpu as pltpu
from jax.sharding import PartitionSpec as P

EPSILON = 1e-06
CODE_RANGE = 448.0
BETA_ONE = 0.9
BETA_TWO = 0.95
LEARN_RATE = 0.01
WEIGHT_DECAY = 0.1
ADAM_EPSILON = 1e-08
steps_done = 10.0
MESH = pl.DeviceIdType.MESH


def quantize(widened):
    most = jnp.max(jnp.abs(widened), axis=-1, keepdims=True)
    scale = ((most + EPSILON) / CODE_RANGE).astype(jnp.bfloat16).astype(jnp.float32)
    codes = (widened / scale).astype(jnp.bfloat16).astype(jnp.float32)
    return codes, scale


def requantized(widened):
    codes, scale = quantize(widened)
    return codes * scale


def adamw(reduced, params, first, second):
    first_next = BETA_ONE * first + (1.0 - BETA_ONE) * reduced
    second_next = BETA_TWO * second + (1.0 - BETA_TWO) * reduced * reduced
    first_hat = first_next / (1.0 - BETA_ONE**steps_done)
    second_hat = second_next / (1.0 - BETA_TWO**steps_done)
    params_next = params - LEARN_RATE * (
        first_hat / (jnp.sqrt(second_hat) + ADAM_EPSILON) + WEIGHT_DECAY * params
    )
    return (params_next, first_next, second_next)


def loop(count, body, carry):
    if count <= 8:
        for step in range(1, count):
            carry = body(step, carry)
        return carry
    return lax.fori_loop(1, count, body, carry)


def everyone(n_inner, n_outer, body):
    if n_inner * n_outer <= 32:
        for place in range(n_inner * n_outer - 1, 0, -1):
            body(place // n_inner, place % n_inner)
    else:

        def step(place, carry):
            body(place // n_inner, place % n_inner)
            return carry

        lax.fori_loop(1, n_inner * n_outer, step, 0)


def arrived(slots, count, sem):
    others = slots.at[pl.ds(1, count - 1)]
    pltpu.make_async_copy(others, others, sem).wait()


def kernel(
    n_inner, n_outer, rows, padded,
    grad_first, grad_second, master, first_moment, second_moment,
    new_master, new_first, new_second, weight_codes, weight_scales,
    stage, spread, blocks, terms, packed, lined, state,
    load_sem, send_one, recv_one, send_two, recv_two,
):
    inner = lax.axis_index("inner")
    outer = lax.axis_index("outer")
    both = 2 * rows
    width = stage.shape[-1]

    def inner_peer(step):
        return lax.rem(inner + step, n_inner)

    def outer_peer(step):
        return lax.rem(outer + step, n_outer)

    grads = [
        pltpu.make_async_copy(ref, stage.at[:, bucket], load_sem.at[bucket])
        for bucket, ref in enumerate((grad_first, grad_second))
    ]
    states = [
        pltpu.make_async_copy(ref, state.at[place], load_sem.at[2 + place])
        for place, ref in enumerate((master, first_moment, second_moment))
    ]
    for copy in grads:
        copy.start()

    barrier = pltpu.get_barrier_semaphore()

    def greet(outer_step, inner_step):
        peer = {"inner": inner_peer(inner_step), "outer": outer_peer(outer_step)}
        pl.semaphore_signal(barrier, inc=1, device_id=peer, device_id_type=MESH)

    everyone(n_inner, n_outer, greet)
    for copy in states:
        copy.start()
    for copy in grads:
        copy.wait()

    spread[...] = stage[...].astype(jnp.float32).reshape(n_inner, both * n_outer, width)

    def gather_rows(place, carry):
        for group in range(n_outer):
            blocks[place, group] = spread[place, pl.ds(group, both, stride=n_outer), :].astype(jnp.bfloat16)
        return carry

    gather_rows(0, 0)
    loop(n_inner, gather_rows, 0)
    pl.semaphore_wait(barrier, n_inner * n_outer - 1)

    def send_term(outer_step, inner_step):
        peer = {"inner": inner_peer(inner_step), "outer": outer_peer(outer_step)}
        pltpu.make_async_remote_copy(
            src_ref=blocks.at[inner_peer(inner_step), outer_peer(outer_step)],
            dst_ref=terms.at[outer_step * n_inner + inner_step],
            send_sem=send_one,
            recv_sem=recv_one,
            device_id=peer,
            device_id_type=MESH,
        ).start()

    everyone(n_inner, n_outer, send_term)
    terms[0] = blocks[inner, outer]
    for copy in states:
        copy.wait()
    params, first, second = (state[place, :, 0] for place in range(3))
    arrived(terms, n_inner * n_outer, recv_one)
    if n_inner * n_outer <= 32:
        arrivals = terms[...].astype(jnp.float32).reshape(n_outer, n_inner, both, width)
        reduced = jnp.sum(requantized(jnp.sum(requantized(arrivals), axis=1)), axis=0)
    else:

        def add_group(group, reduced):
            arrivals = terms[pl.ds(group * n_inner, n_inner)].astype(jnp.float32)
            return reduced + requantized(jnp.sum(requantized(arrivals), axis=0))

        reduced = lax.fori_loop(0, n_outer, add_group, jnp.zeros((both, width), jnp.float32))

    params_next, first_next, second_next = adamw(reduced, params, first, second)
    codes, scale = quantize(params_next)
    lane = lax.broadcasted_iota(jnp.int32, (both, width), 1)
    across = jnp.where(lane == inner, scale, 0.0)
    fill = jnp.zeros((padded - 2 * both, width), jnp.float32)
    packed[inner] = jnp.concatenate([codes, across, fill], axis=0).astype(jnp.bfloat16)

    def send_weight(step, carry):
        pltpu.make_async_remote_copy(
            src_ref=packed.at[inner],
            dst_ref=packed.at[inner],
            send_sem=send_two,
            recv_sem=recv_two,
            device_id={"inner": inner_peer(step)},
            device_id_type=MESH,
        ).start()
        return carry

    loop(n_inner, send_weight, 0)
    new_master[:, 0] = params_next
    new_first[:, 0] = first_next
    new_second[:, 0] = second_next
    arrived(terms, n_inner * n_outer, send_one)
    arrived(packed, n_inner, send_two)
    arrived(packed, n_inner, recv_two)
    gathered = packed[...].astype(jnp.float32)
    lined[...] = gathered.reshape(n_inner * padded, width)
    for place in range(both):
        weight_codes[place] = lined[pl.ds(place, n_inner, stride=padded), :].astype(jnp.bfloat16)
    scales = jnp.sum(gathered[:, both : 2 * both], axis=0)
    for bucket in range(2):
        weight_scales[:, bucket] = scales[bucket * rows : (bucket + 1) * rows, :n_inner].astype(jnp.bfloat16)


def place_kernel(*refs):
    sources, results, sem = refs[:5], refs[5:10], refs[10]
    copies = [
        pltpu.make_async_copy(source, result, sem.at[place])
        for place, (source, result) in enumerate(zip(sources, results))
    ]
    for copy in copies:
        copy.start()
    for copy in copies:
        copy.wait()


def local(n_inner, n_outer, grad_first, grad_second, master, first_moment, second_moment):
    rows, width = grad_first.shape[-2:]
    both = 2 * rows
    padded = 16 * ((2 * both + 15) // 16)
    owned = jax.ShapeDtypeStruct((both, 1, width), jnp.float32)
    shapes = (
        owned,
        owned,
        owned,
        jax.ShapeDtypeStruct((both, n_inner, width), jnp.bfloat16),
        jax.ShapeDtypeStruct((rows, 2, n_inner), jnp.bfloat16),
    )
    hbm = pl.BlockSpec(memory_space=pl.ANY)
    vmem = pl.BlockSpec(memory_space=pltpu.VMEM)
    dma = pltpu.SemaphoreType.DMA
    results = pl.pallas_call(
        functools.partial(kernel, n_inner, n_outer, rows, padded),
        out_shape=shapes,
        in_specs=[pl.BlockSpec(memory_space=pltpu.HBM)] * 5,
        out_specs=(vmem,) * 5,
        scratch_shapes=[
            pltpu.VMEM((n_inner, 2, rows * n_outer, width), jnp.bfloat16),
            pltpu.VMEM((n_inner, both * n_outer, width), jnp.float32),
            pltpu.VMEM((n_inner, n_outer, both, width), jnp.bfloat16),
            pltpu.VMEM((n_inner * n_outer, both, width), jnp.bfloat16),
            pltpu.VMEM((n_inner, padded, width), jnp.bfloat16),
            pltpu.VMEM((n_inner * padded, width), jnp.float32),
            pltpu.VMEM((3, both, 1, width), jnp.float32),
            dma((5,)),
            dma, dma, dma, dma,
        ],
        compiler_params=pltpu.CompilerParams(
            collective_id=0, has_side_effects=True
        ),
        name="reduce_update_gather",
    )(
        jnp.swapaxes(grad_first[0, 0], 1, 2).reshape(n_inner, rows * n_outer, width),
        jnp.swapaxes(grad_second[0, 0], 1, 2).reshape(n_inner, rows * n_outer, width),
        master.reshape(both, 1, width),
        first_moment.reshape(both, 1, width),
        second_moment.reshape(both, 1, width),
    )
    results = pl.pallas_call(
        place_kernel,
        out_shape=shapes,
        in_specs=[vmem] * 5,
        out_specs=(hbm,) * 5,
        scratch_shapes=[dma((5,))],
        name="place_results",
    )(*results)
    new_master, new_first, new_second, weight_codes, weight_scales = results
    state_shape = (2, 1, 1, rows, width)
    return (
        new_master.reshape(state_shape),
        new_first.reshape(state_shape),
        new_second.reshape(state_shape),
        jnp.swapaxes(weight_codes.reshape(2, rows, n_inner, width), 1, 2)[:, :, None],
        jnp.transpose(weight_scales, (1, 2, 0))[:, :, None],
    )


def solution(mesh):
    return jax.shard_map(
        functools.partial(local, mesh.shape["inner"], mesh.shape["outer"]),
        mesh=mesh,
        in_specs=(
            P("outer", "inner", None, None, None, None),
            P("outer", "inner", None, None, None, None),
            P(None, "inner", "outer", None, None),
            P(None, "inner", "outer", None, None),
            P(None, "inner", "outer", None, None),
        ),
        out_specs=(
            P(None, "inner", "outer", None, None),
            P(None, "inner", "outer", None, None),
            P(None, "inner", "outer", None, None),
            P(None, None, "outer", None, None),
            P(None, None, "outer", None),
        ),
        check_vma=False,
    )
```

```python
import functools

import jax
import jax.numpy as jnp
from jax import lax
from jax.experimental import pallas as pl
from jax.experimental.pallas import tpu as pltpu
from jax.sharding import PartitionSpec as P

EPSILON = 1e-06
CODE_RANGE = 448.0
BETA_ONE = 0.9
BETA_TWO = 0.95
LEARN_RATE = 0.01
WEIGHT_DECAY = 0.1
ADAM_EPSILON = 1e-08
steps_done = 10.0
MESH = pl.DeviceIdType.MESH


def quantize(widened):
    most = jnp.max(jnp.abs(widened), axis=-1, keepdims=True)
    scale = ((most + EPSILON) / CODE_RANGE).astype(jnp.bfloat16).astype(jnp.float32)
    codes = (widened / scale).astype(jnp.bfloat16).astype(jnp.float32)
    return codes, scale


def requantized(widened):
    codes, scale = quantize(widened)
    return codes * scale


def adamw(reduced, params, first, second):
    first_next = BETA_ONE * first + (1.0 - BETA_ONE) * reduced
    second_next = BETA_TWO * second + (1.0 - BETA_TWO) * reduced * reduced
    first_hat = first_next / (1.0 - BETA_ONE**steps_done)
    second_hat = second_next / (1.0 - BETA_TWO**steps_done)
    params_next = params - LEARN_RATE * (
        first_hat / (jnp.sqrt(second_hat) + ADAM_EPSILON) + WEIGHT_DECAY * params
    )
    return (params_next, first_next, second_next)


def loop(count, body, carry):
    if count <= 8:
        for step in range(1, count):
            carry = body(step, carry)
        return carry
    return lax.fori_loop(1, count, body, carry)


def everyone(n_inner, n_outer, body):
    if n_inner * n_outer <= 32:
        for place in range(n_inner * n_outer - 1, 0, -1):
            body(place // n_inner, place % n_inner)
    else:

        def step(place, carry):
            body(place // n_inner, place % n_inner)
            return carry

        lax.fori_loop(1, n_inner * n_outer, step, 0)


def arrived(slots, count, sem):
    others = slots.at[pl.ds(1, count - 1)]
    pltpu.make_async_copy(others, others, sem).wait()


def kernel(
    n_inner, n_outer, rows, padded,
    grad_first, grad_second, master, first_moment, second_moment,
    new_master, new_first, new_second, weight_codes, weight_scales,
    stage, spread, blocks, terms, packed, lined, state,
    load_sem, send_one, recv_one, send_two, recv_two,
):
    inner = lax.axis_index("inner")
    outer = lax.axis_index("outer")
    both = 2 * rows
    width = stage.shape[-1]

    few = n_inner * n_outer <= 32
    inner_peers = [lax.rem(inner + step, n_inner) for step in range(n_inner if few else 0)]
    outer_peers = [lax.rem(outer + step, n_outer) for step in range(n_outer if few else 0)]

    def inner_peer(step):
        return inner_peers[step] if few else lax.rem(inner + step, n_inner)

    def outer_peer(step):
        return outer_peers[step] if few else lax.rem(outer + step, n_outer)

    grads = [
        pltpu.make_async_copy(ref, stage.at[:, bucket], load_sem.at[bucket])
        for bucket, ref in enumerate((grad_first, grad_second))
    ]
    states = [
        pltpu.make_async_copy(ref, state.at[place], load_sem.at[2 + place])
        for place, ref in enumerate((master, first_moment, second_moment))
    ]
    for copy in grads:
        copy.start()

    barrier = pltpu.get_barrier_semaphore()

    def greet(outer_step, inner_step):
        peer = {"inner": inner_peer(inner_step), "outer": outer_peer(outer_step)}
        pl.semaphore_signal(barrier, inc=1, device_id=peer, device_id_type=MESH)

    everyone(n_inner, n_outer, greet)
    for copy in states:
        copy.start()
    for copy in grads:
        copy.wait()

    spread[...] = stage[...].astype(jnp.float32).reshape(n_inner, both * n_outer, width)

    def gather_rows(place, carry):
        for group in range(n_outer):
            blocks[place, group] = spread[place, pl.ds(group, both, stride=n_outer), :].astype(jnp.bfloat16)
        return carry

    gather_rows(0, 0)
    loop(n_inner, gather_rows, 0)
    pl.semaphore_wait(barrier, n_inner * n_outer - 1)

    def send_term(outer_step, inner_step):
        peer = {"inner": inner_peer(inner_step), "outer": outer_peer(outer_step)}
        pltpu.make_async_remote_copy(
            src_ref=blocks.at[inner_peer(inner_step), outer_peer(outer_step)],
            dst_ref=terms.at[outer_step * n_inner + inner_step],
            send_sem=send_one,
            recv_sem=recv_one,
            device_id=peer,
            device_id_type=MESH,
        ).start()

    everyone(n_inner, n_outer, send_term)
    terms[0] = blocks[inner, outer]
    for copy in states:
        copy.wait()
    params, first, second = (state[place, :, 0] for place in range(3))
    arrived(terms, n_inner * n_outer, recv_one)
    if n_inner * n_outer <= 32:
        arrivals = terms[...].astype(jnp.float32).reshape(n_outer, n_inner, both, width)
        reduced = jnp.sum(requantized(jnp.sum(requantized(arrivals), axis=1)), axis=0)
    else:

        def add_group(group, reduced):
            arrivals = terms[pl.ds(group * n_inner, n_inner)].astype(jnp.float32)
            return reduced + requantized(jnp.sum(requantized(arrivals), axis=0))

        reduced = lax.fori_loop(0, n_outer, add_group, jnp.zeros((both, width), jnp.float32))

    params_next, first_next, second_next = adamw(reduced, params, first, second)
    codes, scale = quantize(params_next)
    lane = lax.broadcasted_iota(jnp.int32, (both, width), 1)
    across = jnp.where(lane == inner, scale, 0.0)
    fill = jnp.zeros((padded - 2 * both, width), jnp.float32)
    packed[inner] = jnp.concatenate([codes, across, fill], axis=0).astype(jnp.bfloat16)

    def send_weight(step, carry):
        pltpu.make_async_remote_copy(
            src_ref=packed.at[inner],
            dst_ref=packed.at[inner],
            send_sem=send_two,
            recv_sem=recv_two,
            device_id={"inner": inner_peer(step)},
            device_id_type=MESH,
        ).start()
        return carry

    loop(n_inner, send_weight, 0)
    new_master[:, 0] = params_next
    new_first[:, 0] = first_next
    new_second[:, 0] = second_next
    arrived(terms, n_inner * n_outer, send_one)
    arrived(packed, n_inner, send_two)
    arrived(packed, n_inner, recv_two)
    gathered = packed[...].astype(jnp.float32)
    lined[...] = gathered.reshape(n_inner * padded, width)
    for place in range(both):
        weight_codes[place] = lined[pl.ds(place, n_inner, stride=padded), :].astype(jnp.bfloat16)
    scales = jnp.sum(gathered[:, both : 2 * both], axis=0)
    for bucket in range(2):
        weight_scales[:, bucket] = scales[bucket * rows : (bucket + 1) * rows, :n_inner].astype(jnp.bfloat16)


def place_kernel(*refs):
    sources, results, sem = refs[:5], refs[5:10], refs[10]
    copies = [
        pltpu.make_async_copy(source, result, sem.at[place])
        for place, (source, result) in enumerate(zip(sources, results))
    ]
    for copy in copies:
        copy.start()
    for copy in copies:
        copy.wait()


def local(n_inner, n_outer, grad_first, grad_second, master, first_moment, second_moment):
    rows, width = grad_first.shape[-2:]
    both = 2 * rows
    padded = 16 * ((2 * both + 15) // 16)
    owned = jax.ShapeDtypeStruct((both, 1, width), jnp.float32)
    shapes = (
        owned,
        owned,
        owned,
        jax.ShapeDtypeStruct((both, n_inner, width), jnp.bfloat16),
        jax.ShapeDtypeStruct((rows, 2, n_inner), jnp.bfloat16),
    )
    hbm = pl.BlockSpec(memory_space=pl.ANY)
    vmem = pl.BlockSpec(memory_space=pltpu.VMEM)
    dma = pltpu.SemaphoreType.DMA
    results = pl.pallas_call(
        functools.partial(kernel, n_inner, n_outer, rows, padded),
        out_shape=shapes,
        in_specs=[pl.BlockSpec(memory_space=pltpu.HBM)] * 5,
        out_specs=(vmem,) * 5,
        scratch_shapes=[
            pltpu.VMEM((n_inner, 2, rows * n_outer, width), jnp.bfloat16),
            pltpu.VMEM((n_inner, both * n_outer, width), jnp.float32),
            pltpu.VMEM((n_inner, n_outer, both, width), jnp.bfloat16),
            pltpu.VMEM((n_inner * n_outer, both, width), jnp.bfloat16),
            pltpu.VMEM((n_inner, padded, width), jnp.bfloat16),
            pltpu.VMEM((n_inner * padded, width), jnp.float32),
            pltpu.VMEM((3, both, 1, width), jnp.float32),
            dma((5,)),
            dma, dma, dma, dma,
        ],
        compiler_params=pltpu.CompilerParams(
            collective_id=0, has_side_effects=True
        ),
        name="reduce_update_gather",
    )(
        jnp.swapaxes(grad_first[0, 0], 1, 2).reshape(n_inner, rows * n_outer, width),
        jnp.swapaxes(grad_second[0, 0], 1, 2).reshape(n_inner, rows * n_outer, width),
        master.reshape(both, 1, width),
        first_moment.reshape(both, 1, width),
        second_moment.reshape(both, 1, width),
    )
    results = pl.pallas_call(
        place_kernel,
        out_shape=shapes,
        in_specs=[vmem] * 5,
        out_specs=(hbm,) * 5,
        scratch_shapes=[dma((5,))],
        name="place_results",
    )(*results)
    new_master, new_first, new_second, weight_codes, weight_scales = results
    state_shape = (2, 1, 1, rows, width)
    return (
        new_master.reshape(state_shape),
        new_first.reshape(state_shape),
        new_second.reshape(state_shape),
        jnp.swapaxes(weight_codes.reshape(2, rows, n_inner, width), 1, 2)[:, :, None],
        jnp.transpose(weight_scales, (1, 2, 0))[:, :, None],
    )


def solution(mesh):
    return jax.shard_map(
        functools.partial(local, mesh.shape["inner"], mesh.shape["outer"]),
        mesh=mesh,
        in_specs=(
            P("outer", "inner", None, None, None, None),
            P("outer", "inner", None, None, None, None),
            P(None, "inner", "outer", None, None),
            P(None, "inner", "outer", None, None),
            P(None, "inner", "outer", None, None),
        ),
        out_specs=(
            P(None, "inner", "outer", None, None),
            P(None, "inner", "outer", None, None),
            P(None, "inner", "outer", None, None),
            P(None, None, "outer", None, None),
            P(None, None, "outer", None),
        ),
        check_vma=False,
    )
```
